32 devices in a mesh: ctx: 8 (over z, y), ch: 4 (over x, core).
Axes of the slice: x: 2, y: 2, z: 4, core: 2. Of those that a mesh axis runs over, the one named last changes fastest.
Arguments:
- query_input: bfloat16 [4096, 2048], P('ctx', 'ch'), may hold values from -6 to 6
- key_input: bfloat16 [4096, 2048], P('ctx', 'ch'), may hold values from -6 to 6
- value_input: bfloat16 [4096, 2048], P('ctx', 'ch'), may hold values from -6 to 6
- filters: bfloat16 [2, 4096], replicated, may hold values from -1 to 1
- cotangent: bfloat16 [4096, 2048], P('ctx', 'ch'), may hold values from -6 to 6
Outputs:
- query_adjoint: bfloat16 [4096, 2048], P('ctx', 'ch')
- key_adjoint: bfloat16 [4096, 2048], P('ctx', 'ch')
- value_adjoint: bfloat16 [4096, 2048], P('ctx', 'ch')
- filter_adjoint: float32 [2, 4096], P(None, 'ctx')
The draws below stay inside these ranges and needn't reach their ends.
All inputs are finite; a program needn't handle non-finite values.
Results may differ from the reference program's by a relative error of at most 0.0051.
Values may be sent and summed in bfloat16 or wider, within the bound.
No kernel may reach another device: no remote copies, remote signals or barrier semaphores. Data moves between devices by JAX's collectives and lax.ppermute only.
A program may use at most 64 MiB of HBM per device.

```python
import math
import jax
import jax.numpy as jnp
from jax import lax

GW = 1024
CHANNELS = 2048
GROUPS = 2
L = 4096


def draw_filters(key, part):
    key = jax.random.fold_in(key, 11)
    subkeys = jax.random.split(key, 3)
    lag_index = jnp.arange(L, dtype=jnp.float32)[None, :]
    near_scale = jax.random.uniform(subkeys[0], (GROUPS, 1), jnp.float32, 30.0, 50.0)
    far_rates = jax.random.uniform(subkeys[1], (GROUPS, 1), jnp.float32, 0.3, 2.0)
    rough_noise = jnp.clip(jax.random.normal(subkeys[2], (GROUPS, L), jnp.float32), -4.0, 4.0)
    envelope = 0.22 * jnp.exp(-lag_index / near_scale) + jnp.exp(-far_rates * lag_index / L) / jnp.sqrt(jnp.float32(L))
    return (rough_noise * envelope).astype(jnp.bfloat16)


def level_of(rng, dims, cuts, least, largest):
    def one(position, parts):
        heights = jax.random.uniform(jax.random.fold_in(jax.random.fold_in(rng, 6), position), (parts,), jnp.float32, least / len(cuts), largest / len(cuts))
        return jnp.repeat(jnp.exp(heights), dims[position] // parts).reshape((-1,) + (1,) * (len(dims) - position - 1))

    level = one(*cuts[0])
    for cut in cuts[1:]:
        level = level * one(*cut)
    return level


def scatter_about(key, shape, scale, bound, cuts=(), held_as=jnp.bfloat16):
    array = jax.random.normal(key, shape, jnp.float32) * scale
    if len(cuts) > 0:
        array = level_of(key, shape, cuts, -0.22, 0.18) * array
    return jnp.clip(array, min=-bound, max=bound).astype(held_as)


def setup_inputs(seed: int = 0) -> dict:
    seeds = jax.random.split(jax.random.key(seed), 6)
    return {
        "query_input": scatter_about(seeds[0], (L, CHANNELS), 1.0, 6.0, ((0, 8), (1, 4))),
        "key_input": scatter_about(seeds[1], (L, CHANNELS), 1.0, 6.0, ((0, 8), (1, 4))),
        "value_input": scatter_about(seeds[2], (L, CHANNELS), 1.0, 6.0, ((0, 8), (1, 4))),
        "filters": draw_filters(jax.random.fold_in(seeds[5], 71), 0),
        "cotangent": scatter_about(seeds[4], (L, CHANNELS), 1.0, 6.0, ((0, 8), (1, 4))),
    }


def reference(query_input, key_input, value_input, filters, cotangent):
    seq_total = query_input.shape[0]
    fft_len = 2 * seq_total
    num_groups = filters.shape[0]
    product = (key_input.astype(jnp.float32) * value_input.astype(jnp.float32)).astype(jnp.bfloat16)
    gated_adj = (cotangent.astype(jnp.float32) * query_input.astype(jnp.float32)).astype(jnp.bfloat16)

    def per_group(group_index):
        input_cols = lax.dynamic_slice_in_dim(product, group_index * GW, GW, 1).astype(jnp.float32)
        adjoint_cols = lax.dynamic_slice_in_dim(gated_adj, group_index * GW, GW, 1).astype(jnp.float32)
        filter_taps = lax.dynamic_index_in_dim(filters, group_index, 0, keepdims=False).astype(jnp.float32)
        filter_spec = jnp.fft.rfft(filter_taps, n=fft_len)[:, None]
        input_spec = jnp.fft.rfft(input_cols, n=fft_len, axis=0)
        adjoint_spec = jnp.fft.rfft(adjoint_cols, n=fft_len, axis=0)
        mixed_cols = jnp.fft.irfft(input_spec * filter_spec, n=fft_len, axis=0)[:seq_total]
        back_cols = jnp.fft.irfft(adjoint_spec * jnp.conj(filter_spec), n=fft_len, axis=0)[:seq_total]
        lagged = jnp.fft.irfft(lax.optimization_barrier(jnp.sum(adjoint_spec * jnp.conj(input_spec), axis=1)), n=fft_len)[:seq_total]
        return (mixed_cols.astype(jnp.float32), back_cols.astype(jnp.float32), lagged.astype(jnp.float32))
    mixed_all, back_all, lagged_all = lax.map(per_group, jnp.arange(num_groups, dtype=jnp.int32))
    mixed = jnp.transpose(mixed_all, (1, 0, 2)).reshape(seq_total, num_groups * GW)
    back = jnp.transpose(back_all, (1, 0, 2)).reshape(seq_total, num_groups * GW)
    query_adjoint = (cotangent.astype(jnp.float32) * mixed).astype(jnp.bfloat16)
    key_adjoint = (back * value_input.astype(jnp.float32)).astype(jnp.bfloat16)
    value_adjoint = (back * key_input.astype(jnp.float32)).astype(jnp.bfloat16)
    filter_adjoint = lagged_all * (1.0 / math.sqrt(seq_total * GW))
    return (query_adjoint, key_adjoint, value_adjoint, filter_adjoint)
```

```python
import functools
import math

import jax
import jax.numpy as jnp
from jax import lax
from jax.experimental import pallas as pl
from jax.experimental.pallas import tpu as pltpu
from jax.sharding import PartitionSpec as P

GW = 1024
LANES = 128
VMEM_LIMIT = 56 * 1024 * 1024
VMEM = pl.BlockSpec(memory_space=pltpu.VMEM)
SMEM = pl.BlockSpec(memory_space=pltpu.SMEM)


def params():
    return pltpu.CompilerParams(vmem_limit_bytes=VMEM_LIMIT)


def f32_product(left, right):
    return left.astype(jnp.float32) * right.astype(jnp.float32)


def split_kernel(owners, place, key, value, query, cot, *outs):
    q, upper = place[0], place[1]
    for k in range(owners):
        lanes = pl.ds(pl.multiple_of((q ^ k) * LANES, LANES), LANES)
        product = f32_product(key[:, lanes], value[:, lanes]).astype(jnp.bfloat16)
        gated = f32_product(cot[:, lanes], query[:, lanes]).astype(jnp.bfloat16)
        outs[k][0] = product
        outs[k][1] = gated
        outs[owners + k][...] = jnp.where(upper == 1, gated, product)


def split_streams(owners, place, key, value, query, cot):
    rows, channels = key.shape
    width = channels // owners
    if width == LANES:
        pair = jax.ShapeDtypeStruct((2, rows, LANES), jnp.bfloat16)
        single = jax.ShapeDtypeStruct((rows, LANES), jnp.bfloat16)
        outs = pl.pallas_call(
            functools.partial(split_kernel, owners),
            out_shape=[pair] * owners + [single] * owners,
            in_specs=[SMEM] + [VMEM] * 4,
            out_specs=[VMEM] * (2 * owners),
            compiler_params=params(),
            name="split_streams",
        )(place, key, value, query, cot)
        return outs[:owners], outs[owners:]
    product = f32_product(key, value).astype(jnp.bfloat16)
    gated = f32_product(cot, query).astype(jnp.bfloat16)
    both = jnp.stack([product, gated]).reshape(2, rows, owners, width)
    both = jnp.pad(both, ((0, 0), (0, 0), (0, 0), (0, LANES - width)))
    pairs = [lax.dynamic_index_in_dim(both, place[0] ^ k, 2, keepdims=False) for k in range(owners)]
    return pairs, [jnp.where(place[1] == 1, pair[1], pair[0]) for pair in pairs]


def tables_kernel(rows_ref, out):
    block, seq = out.shape[1], out.shape[2]
    sub = lax.broadcasted_iota(jnp.int32, (8, rows_ref.shape[1]), 0)
    width = rows_ref.shape[1]
    for which in range(2):
        eight = jnp.broadcast_to(rows_ref[which : which + 1, :], (8, width))
        for bit in (1, 2, 4):
            eight = jnp.where((sub & bit) != 0, pltpu.roll(eight, bit, 1), eight)
        for pair in range(block // 16):
            low = pltpu.roll(eight, 16 * pair, 1) if pair else eight
            high = pltpu.roll(eight, 16 * pair + 8, 1)
            both = jnp.concatenate([low[:, :seq], high[:, :seq]], axis=0)
            out[which, 16 * pair : 16 * pair + 16, :] = both.astype(jnp.bfloat16)


def toeplitz_tables(taps, block):
    seq = taps.shape[0]
    zeros = jnp.zeros((block,), jnp.float32)
    taps = taps.astype(jnp.float32)
    down = jnp.concatenate([taps[::-1], zeros])
    down = jnp.concatenate([down[block - 1 :], down[: block - 1]])
    rows = jnp.stack([down, jnp.concatenate([taps, zeros])])
    return pl.pallas_call(
        tables_kernel,
        out_shape=jax.ShapeDtypeStruct((2, block, seq), jnp.bfloat16),
        in_specs=[VMEM],
        out_specs=VMEM,
        compiler_params=params(),
        name="toeplitz_tables",
    )(rows)


def lags_kernel(owners, place, *refs):
    halves, crossing = refs[:owners], refs[owners : 2 * owners]
    out, lane_blocks, sums = refs[2 * owners :]
    q, upper = place[0], place[1]
    block = halves[0].shape[1] // 2
    half_blocks = 2 * owners
    blocks = 2 * half_blocks
    lane_blocks[:, 2 * blocks * LANES :] = jnp.zeros((block, LANES), jnp.bfloat16)
    for k in range(owners):
        near = upper * half_blocks + 2 * (q ^ k)
        far = 2 * (q ^ k) + jnp.where(upper == 1, 0, blocks + half_blocks)
        for part in range(2):
            rows = slice(part * block, (part + 1) * block)
            for which in range(2):
                start = pl.multiple_of((near + which * blocks + part) * LANES, LANES)
                lane_blocks[:, pl.ds(start, LANES)] = halves[k][which, rows, :]
            start = pl.multiple_of((far + part) * LANES, LANES)
            lane_blocks[:, pl.ds(start, LANES)] = crossing[k][rows, :]
    for lag in range(blocks):
        count = (blocks - lag + 1) // 2
        first = jnp.where(upper == 1, count, 0)
        left = lane_blocks[:, pl.ds(pl.multiple_of(first * LANES, LANES), count * LANES)]
        start = pl.multiple_of((first + lag + blocks) * LANES, LANES)
        right = lane_blocks[:, pl.ds(start, count * LANES)]
        sums[lag] = lax.dot_general(
            left, right, (((1,), (1,)), ((), ())), preferred_element_type=jnp.float32
        )
    sums[blocks] = jnp.zeros((block, block), jnp.float32)
    steps = block // LANES

    def diagonal(lag):
        total = None
        for a in range(steps):
            b = lag + a
            rows = slice(a * LANES, (a + 1) * LANES)
            cols = slice((b % steps) * LANES, (b % steps + 1) * LANES)
            tile = sums[b // steps, rows, cols]
            total = tile if total is None else total + tile
        return total

    row = lax.broadcasted_iota(jnp.int32, (LANES, LANES), 0)
    col = lax.broadcasted_iota(jnp.int32, (LANES, LANES), 1)
    sub = lax.broadcasted_iota(jnp.int32, (8, LANES), 0)
    current = diagonal(0)
    for lag in range(steps * blocks):
        after = diagonal(lag + 1) if lag + 1 < steps * blocks else jnp.zeros_like(current)
        mixed = jnp.where(col >= row, current, after)
        eight = mixed[:8]
        for m in range(1, LANES // 8):
            eight = eight + pltpu.roll(mixed[8 * m : 8 * m + 8], LANES - 8 * m, 1)
        for bit in (1, 2, 4):
            eight = jnp.where((sub & bit) != 0, pltpu.roll(eight, LANES - bit, 1), eight)
        out[lag : lag + 1, :] = jnp.sum(eight, axis=0, keepdims=True)
        current = after


def lag_sums(owners, place, halves, crossing):
    block = halves[0].shape[1] // 2
    blocks = 4 * owners
    return pl.pallas_call(
        functools.partial(lags_kernel, owners),
        out_shape=jax.ShapeDtypeStruct((blocks * block // LANES, LANES), jnp.float32),
        in_specs=[SMEM] + [VMEM] * (2 * owners),
        out_specs=VMEM,
        scratch_shapes=[
            pltpu.VMEM((block, (2 * blocks + 1) * LANES), jnp.bfloat16),
            pltpu.VMEM((blocks + 1, block, block), jnp.float32),
        ],
        compiler_params=params(),
        name="lag_sums",
    )(place, *halves, *crossing)


def conv_kernel(owners, place, tables, *refs):
    halves, crossing = refs[:owners], refs[owners : 2 * owners]
    outs = refs[2 * owners : 3 * owners]
    whole, half, results = refs[3 * owners :]
    q, upper = place[0], place[1]
    rows = halves[0].shape[1]
    block = rows // 2
    half_blocks = 2 * owners
    blocks = 2 * half_blocks
    zeros = jnp.zeros((block, LANES), jnp.bfloat16)
    for ref, count in ((whole, blocks), (half, half_blocks)):
        ref[:block] = zeros
        ref[(count + 1) * block :] = zeros
    for k in range(owners):
        start = block + (q ^ k) * rows
        near = pl.multiple_of(start + upper * half_blocks * block, block)
        far = pl.multiple_of(start + (1 - upper) * half_blocks * block, block)
        own, other = halves[k][1 - upper], halves[k][upper]
        whole[pl.ds(near, rows), :] = own
        whole[pl.ds(far, rows), :] = crossing[k][...]
        half[pl.ds(pl.multiple_of(start, block), rows), :] = other
    for ref, count, table, slot in (
        (whole, half_blocks, 1 - upper, 1 - upper),
        (half, 0, upper, upper),
    ):
        for i in range(owners):
            depth = (count + 2 * i + 2) * block
            down = (blocks * block - depth) * (1 - table)
            first = table * (half_blocks - 1 - 2 * i) * block
            window = tables[table, :, pl.ds(pl.multiple_of(down, block), depth)]
            first = pl.multiple_of(first, block)
            pair = jnp.concatenate(
                [ref[pl.ds(first, depth), :], ref[pl.ds(first + block, depth), :]], axis=1
            )
            got = jnp.dot(window, pair, preferred_element_type=jnp.float32).astype(jnp.bfloat16)
            to = jnp.where(table == 0, i, owners - 1 - i)
            results[to, slot, :block, :] = got[:, :LANES]
            results[to, slot, block:, :] = got[:, LANES:]
    for k in range(owners):
        outs[k][...] = results[q ^ k]


def convolve(owners, place, tables, halves, crossing):
    rows = halves[0].shape[1]
    block = rows // 2
    seq = tables.shape[2]
    pair = jax.ShapeDtypeStruct((2, rows, LANES), jnp.bfloat16)
    return pl.pallas_call(
        functools.partial(conv_kernel, owners),
        out_shape=[pair] * owners,
        in_specs=[SMEM] + [VMEM] * (2 * owners + 1),
        out_specs=[VMEM] * owners,
        scratch_shapes=[
            pltpu.VMEM((seq + 2 * block, LANES), jnp.bfloat16),
            pltpu.VMEM((seq // 2 + 2 * block, LANES), jnp.bfloat16),
            pltpu.VMEM((owners, 2, rows, LANES), jnp.bfloat16),
        ],
        compiler_params=params(),
        name="convolve",
    )(place, tables, *halves, *crossing)


def adjoints_kernel(owners, place, key, value, cot, *refs):
    parts = refs[:owners]
    query_adj, key_adj, value_adj = refs[owners:]
    for k in range(owners):
        lanes = pl.ds(pl.multiple_of((place[0] ^ k) * LANES, LANES), LANES)
        mixed, back = parts[k][0], parts[k][1]
        query_adj[:, lanes] = f32_product(cot[:, lanes], mixed).astype(jnp.bfloat16)
        key_adj[:, lanes] = f32_product(back, value[:, lanes]).astype(jnp.bfloat16)
        value_adj[:, lanes] = f32_product(back, key[:, lanes]).astype(jnp.bfloat16)


def adjoints(owners, place, key, value, cot, parts):
    rows, channels = key.shape
    width = channels // owners
    if width == LANES:
        return pl.pallas_call(
            functools.partial(adjoints_kernel, owners),
            out_shape=[jax.ShapeDtypeStruct((rows, channels), jnp.bfloat16)] * 3,
            in_specs=[SMEM] + [VMEM] * (3 + owners),
            out_specs=[VMEM] * 3,
            compiler_params=params(),
            name="adjoints",
        )(place, key, value, cot, *parts)
    both = jnp.zeros((2, rows, channels), jnp.bfloat16)
    for k in range(owners):
        start = (place[0] ^ k) * width
        both = lax.dynamic_update_slice_in_dim(both, parts[k][:, :, :width], start, 2)
    return tuple(
        f32_product(left, right).astype(jnp.bfloat16)
        for left, right in ((cot, both[0]), (both[1], value), (both[1], key))
    )


def on_device(size, ch_size, query, key, value, filters, cot):
    rows, channels = query.shape
    groups, seq = filters.shape
    owners = size // 2
    me = lax.axis_index("ctx")
    place = jnp.stack([me % owners, me // owners]).astype(jnp.int32)
    ch = lax.axis_index("ch")
    group = ch * channels // GW
    sharing = GW // channels

    def swap(array, axis, count, bits):
        return lax.ppermute(array, axis, [(i, i ^ bits) for i in range(count)])

    pairs, singles = split_streams(owners, place, key, value, query, cot)
    halves = [pairs[0]] + [swap(pairs[k], "ctx", size, k) for k in range(1, owners)]
    crossing = [swap(singles[k], "ctx", size, owners ^ k) for k in range(owners)]
    taps = lax.dynamic_index_in_dim(filters, group, 0, keepdims=False)
    tables = toeplitz_tables(taps, rows // 2)
    lags = lag_sums(owners, place, halves, crossing)
    parts = convolve(owners, place, tables, halves, crossing)
    parts = [parts[0]] + [swap(parts[k], "ctx", size, k) for k in range(1, owners)]
    outs = adjoints(owners, place, key, value, cot, parts)

    lags = lags.reshape(size, rows) * (1.0 / math.sqrt(seq * GW))
    bits = 1
    while bits < sharing:
        lags = lags + swap(lags, "ch", ch_size, bits)
        bits *= 2
    span = size // 2
    while span:
        mine = (me // span) % 2
        keep = lax.dynamic_slice_in_dim(lags, mine * span, span, 0)
        give = lax.dynamic_slice_in_dim(lags, (1 - mine) * span, span, 0)
        lags = keep + swap(give, "ctx", size, span)
        span //= 2
    spread = jnp.where(jnp.arange(groups, dtype=jnp.int32)[:, None] == group, lags, 0.0)
    while bits < ch_size:
        spread = spread + swap(spread, "ch", ch_size, bits)
        bits *= 2
    return (*outs, spread)


def solution(mesh):
    return jax.shard_map(
        functools.partial(on_device, mesh.shape["ctx"], mesh.shape["ch"]),
        mesh=mesh,
        in_specs=(P("ctx", "ch"), P("ctx", "ch"), P("ctx", "ch"), P(), P("ctx", "ch")),
        out_specs=(P("ctx", "ch"), P("ctx", "ch"), P("ctx", "ch"), P(None, "ctx")),
        check_vma=False,
    )
```

```python
import functools
import math

import jax
import jax.numpy as jnp
from jax import lax
from jax.experimental import pallas as pl
from jax.experimental.pallas import tpu as pltpu
from jax.sharding import PartitionSpec as P

GW = 1024
LANES = 128
VMEM_LIMIT = 13 * 1024 * 1024
WHOLE_VMEM = 60 * 1024 * 1024
VMEM = pl.BlockSpec(memory_space=pltpu.VMEM)
ANY = pl.BlockSpec(memory_space=pl.ANY)


def params(limit=VMEM_LIMIT):
    return pltpu.CompilerParams(vmem_limit_bytes=limit)


def whereabouts(owners):
    me = lax.axis_index("ctx")
    return me % owners, me // owners


def f32_product(left, right):
    return left.astype(jnp.float32) * right.astype(jnp.float32)


def cost(flops, moved):
    return pl.CostEstimate(flops=2 * flops, bytes_accessed=moved, transcendentals=0)


def split_kernel(owners, *refs):
    streams, outs, held, sems = refs[:4], refs[4 : 5 + owners], refs[-2], refs[-1]
    q, upper = whereabouts(owners)
    rows = streams[0].shape[0]
    pieces = held.shape[1]
    span = rows // pieces
    copies = []
    for p in range(pieces):
        for i in range(4):
            copy = pltpu.make_async_copy(
                streams[i].at[pl.ds(p * span, span), :], held.at[i, p], sems.at[i, p]
            )
            copy.start()
            copies.append(copy)
    for p in range(pieces):
        for copy in copies[4 * p : 4 * p + 4]:
            copy.wait()
        here = slice(p * span, (p + 1) * span)
        for k in range(owners):
            lanes = pl.ds(pl.multiple_of((q ^ k) * LANES, LANES), LANES)
            key, value, query, cot = (held[i, p, :, lanes] for i in range(4))
            product = f32_product(key, value).astype(jnp.bfloat16)
            gated = f32_product(cot, query).astype(jnp.bfloat16)
            outs[k][0, here, :] = product
            outs[k][1, here, :] = gated
            if k == 0:
                outs[owners][here, :] = jnp.where(upper == 1, gated, product)


def split_streams(owners, key, value, query, cot):
    rows, channels = key.shape
    width = channels // owners
    if width == LANES:
        pair = jax.ShapeDtypeStruct((2, rows, LANES), jnp.bfloat16)
        single = jax.ShapeDtypeStruct((rows, LANES), jnp.bfloat16)
        outs = pl.pallas_call(
            functools.partial(split_kernel, owners),
            out_shape=[pair] * owners + [single],
            in_specs=[ANY] * 4,
            out_specs=[VMEM] * (owners + 1),
            scratch_shapes=[
                pltpu.VMEM((4, 4, rows // 4, channels), jnp.bfloat16),
                pltpu.SemaphoreType.DMA((4, 4)),
            ],
            compiler_params=params(WHOLE_VMEM),
            name="split_streams",
        )(key, value, query, cot)
        return outs[:owners], outs[owners]
    q, upper = whereabouts(owners)
    product = f32_product(key, value).astype(jnp.bfloat16)
    gated = f32_product(cot, query).astype(jnp.bfloat16)
    both = jnp.stack([product, gated]).reshape(2, rows, owners, width)
    both = jnp.pad(both, ((0, 0), (0, 0), (0, 0), (0, LANES - width)))
    pairs = [lax.dynamic_index_in_dim(both, q ^ k, 2, keepdims=False) for k in range(owners)]
    return pairs, jnp.where(upper == 1, pairs[0][1], pairs[0][0])


def fill_table(row, out):
    block, seq = out.shape
    width = row.shape[1]
    sub = lax.broadcasted_iota(jnp.int32, (8, width), 0)
    eight = jnp.broadcast_to(row, (8, width))
    for bit in (1, 2, 4):
        eight = jnp.where((sub & bit) != 0, pltpu.roll(eight, bit, 1), eight)
    for start in range(0, block, 16):
        low = pltpu.roll(eight, start, 1) if start else eight
        high = pltpu.roll(eight, start + 8, 1)
        both = jnp.concatenate([low[:, :seq], high[:, :seq]], axis=0)
        out[start : start + 16, :] = both.astype(jnp.bfloat16)


def table_rows(taps, block):
    zeros = jnp.zeros((block,), jnp.float32)
    taps = taps.astype(jnp.float32)
    down = jnp.concatenate([taps[::-1], zeros])
    down = jnp.concatenate([down[block - 1 :], down[: block - 1]])
    return jnp.stack([down, jnp.concatenate([taps, zeros])])


def tail_rows(rows):
    return -(-2 * rows // (16 * LANES)) * 16


def to_tail(lags, rows):
    high = lax.reduce_precision(lags, 8, 7)
    low = (lags - high).astype(jnp.bfloat16)
    high = high.astype(jnp.bfloat16)
    flat = jnp.concatenate([high.reshape(-1, LANES), low.reshape(-1, LANES)])
    return jnp.pad(flat, ((0, tail_rows(rows) - flat.shape[0]), (0, 0)))


def from_tail(part, rows):
    count = rows // LANES
    pairs = part[rows : rows + 2 * count].astype(jnp.float32)
    return (pairs[:count] + pairs[count:]).reshape(rows)


def fold_diagonals(sums, out):
    blocks, block = sums.shape[0], sums.shape[1]
    steps = block // LANES

    def diagonal(lag):
        total = None
        for a in range(steps):
            b = lag + a
            if b // steps < blocks:
                rows = slice(a * LANES, (a + 1) * LANES)
                cols = slice((b % steps) * LANES, (b % steps + 1) * LANES)
                tile = sums[b // steps, rows, cols]
                total = tile if total is None else total + tile
        return jnp.zeros((LANES, LANES), jnp.float32) if total is None else total

    row = lax.broadcasted_iota(jnp.int32, (LANES, LANES), 0)
    col = lax.broadcasted_iota(jnp.int32, (LANES, LANES), 1)
    sub = lax.broadcasted_iota(jnp.int32, (8, LANES), 0)
    current = diagonal(0)
    for lag in range(out.shape[0]):
        after = diagonal(lag + 1)
        mixed = jnp.where(col >= row, current, after)
        eight = mixed[:8]
        for m in range(1, LANES // 8):
            eight = eight + pltpu.roll(mixed[8 * m : 8 * m + 8], LANES - 8 * m, 1)
        for bit in (1, 2, 4):
            eight = jnp.where((sub & bit) != 0, pltpu.roll(eight, LANES - bit, 1), eight)
        out[lag : lag + 1, :] = jnp.sum(eight, axis=0, keepdims=True)
        current = after


def cross_rows(left, right):
    return lax.dot_general(
        left, right, (((1,), (1,)), ((), ())), preferred_element_type=jnp.float32
    )


def far_lags_kernel(owners, scale, *refs):
    halves, crossing = refs[:owners], refs[owners : 2 * owners]
    out, lane_blocks, sums = refs[2 * owners :]
    q, upper = whereabouts(owners)
    block = halves[0].shape[1] // 2
    half_blocks = 2 * owners
    for k in range(owners):
        for part in range(2):
            rows = slice(part * block, (part + 1) * block)
            lanes = pl.ds(pl.multiple_of((2 * (q ^ k) + part) * LANES, LANES), LANES)
            lane_blocks[upper, :, lanes] = halves[k][upper, rows, :]
            lane_blocks[1 - upper, :, lanes] = crossing[k][rows, :]
    sums[half_blocks * upper] = jnp.zeros((block, block), jnp.float32)
    for i in range(half_blocks):
        count = (half_blocks - i) * LANES
        left = pl.ds(pl.multiple_of((1 - upper) * i * LANES, LANES), count)
        right = pl.ds(pl.multiple_of(upper * i * LANES, LANES), count)
        lag = jnp.where(upper == 1, i, half_blocks - i)
        sums[lag] = cross_rows(lane_blocks[0, :, left], lane_blocks[1, :, right])
    fold_diagonals(sums, out)
    out[...] *= scale


def far_lags(owners, scale, halves, crossing):
    block = halves[0].shape[1] // 2
    half_blocks = 2 * owners
    return pl.pallas_call(
        functools.partial(far_lags_kernel, owners, scale),
        out_shape=jax.ShapeDtypeStruct((half_blocks * block // LANES, LANES), jnp.float32),
        in_specs=[VMEM] * (2 * owners),
        out_specs=VMEM,
        scratch_shapes=[
            pltpu.VMEM((2, block, half_blocks * LANES), jnp.bfloat16),
            pltpu.VMEM((half_blocks + 1, block, block), jnp.float32),
        ],
        compiler_params=params(),
        cost_estimate=cost(1 << 20, 1 << 16),
        name="far_lags",
    )(*halves, *crossing)


def near_kernel(owners, scale, firsts, *refs):
    halves = refs[:owners]
    early = refs[owners : 2 * owners]
    main, near_lags, results, streams, lane_blocks, sums, tables = refs[2 * owners :]
    for which in range(2):
        fill_table(firsts[which : which + 1, :], tables.at[which])
    q, upper = whereabouts(owners)
    rows = halves[0].shape[1]
    block = rows // 2
    half_blocks = 2 * owners
    zeros = jnp.zeros((2, block, LANES), jnp.bfloat16)
    streams[:, :block] = zeros
    streams[:, (half_blocks + 1) * block :] = zeros
    for k in range(owners):
        start = pl.multiple_of(block + (q ^ k) * rows, block)
        streams[:, pl.ds(start, rows), :] = halves[k][...]
        for part in range(2):
            lanes = pl.ds(pl.multiple_of((2 * (q ^ k) + part) * LANES, LANES), LANES)
            lane_blocks[:, :, lanes] = halves[k][:, part * block : (part + 1) * block, :]
    for which in range(2):
        for i in range(owners):
            depth = (2 * i + 2) * block
            if which == 0:
                window = tables[0, :, tables.shape[2] - depth :]
                first, to = 0, i
            else:
                window = tables[1, :, :depth]
                first, to = (half_blocks - 1 - 2 * i) * block, owners - 1 - i
            pair = jnp.concatenate(
                [
                    streams[which, first : first + depth, :],
                    streams[which, first + block : first + block + depth, :],
                ],
                axis=1,
            )
            got = jnp.dot(window, pair, preferred_element_type=jnp.float32)
            results[which, to, :block, :] = got[:, :LANES]
            results[which, to, block:, :] = got[:, LANES:]
    for k in range(owners):
        early[k][...] = results[upper, q ^ k].astype(jnp.bfloat16)
    main[...] = results[1 - upper]
    for lag in range(half_blocks):
        count = (half_blocks - lag) * LANES
        sums[lag] = cross_rows(
            lane_blocks[0, :, :count], lane_blocks[1, :, lag * LANES : lag * LANES + count]
        )
    fold_diagonals(sums, near_lags)
    near_lags[...] *= scale


def near(owners, scale, firsts, halves):
    rows = halves[0].shape[1]
    block = rows // 2
    half_blocks = 2 * owners
    single = jax.ShapeDtypeStruct((rows, LANES), jnp.bfloat16)
    outs = pl.pallas_call(
        functools.partial(near_kernel, owners, scale),
        out_shape=[single] * owners
        + [
            jax.ShapeDtypeStruct((owners, rows, LANES), jnp.float32),
            jax.ShapeDtypeStruct((half_blocks * block // LANES, LANES), jnp.float32),
        ],
        in_specs=[VMEM] * (owners + 1),
        out_specs=[VMEM] * (owners + 2),
        scratch_shapes=[
            pltpu.VMEM((2, owners, rows, LANES), jnp.float32),
            pltpu.VMEM((2, (half_blocks + 2) * block, LANES), jnp.bfloat16),
            pltpu.VMEM((2, block, half_blocks * LANES), jnp.bfloat16),
            pltpu.VMEM((half_blocks, block, block), jnp.float32),
            pltpu.VMEM((2, block, firsts.shape[1] - block), jnp.bfloat16),
        ],
        compiler_params=params(),
        cost_estimate=cost(3 * half_blocks * half_blocks * block * block * LANES, 8 << 20),
        name="near",
    )(firsts, *halves)
    return outs[:owners], outs[owners], outs[owners + 1]


def far_kernel(owners, firsts, main, *refs):
    crossing, outs = refs[:owners], refs[owners : 2 * owners]
    stream, results, table = refs[2 * owners :]
    q, upper = whereabouts(owners)
    rows = crossing[0].shape[0]
    block = rows // 2
    half_blocks = 2 * owners
    zeros = jnp.zeros((block, LANES), jnp.bfloat16)
    stream[:block] = zeros
    stream[(half_blocks + 1) * block :] = zeros
    for k in range(owners):
        start = pl.multiple_of(block + (q ^ k) * rows, block)
        stream[pl.ds(start, rows), :] = crossing[k][...]
    fill_table(firsts[pl.ds(1 - upper, 1), :], table)
    depth = (half_blocks + 1) * block
    for i in range(owners):
        start = jnp.where(upper == 1, half_blocks - 2 - 2 * i, 1 + 2 * i) * block
        window = table[:, pl.ds(pl.multiple_of(start, block), depth)]
        pair = jnp.concatenate([stream[:depth, :], stream[block : block + depth, :]], axis=1)
        got = jnp.dot(window, pair, preferred_element_type=jnp.float32)
        to = jnp.where(upper == 1, i, owners - 1 - i)
        low = main[to, :block, :] + got[:, :LANES]
        high = main[to, block:, :] + got[:, LANES:]
        results[to, :block, :] = low.astype(jnp.bfloat16)
        results[to, block:, :] = high.astype(jnp.bfloat16)
    for k in range(owners):
        outs[k][:rows, :] = results[q ^ k]
        outs[k][rows:, :] = jnp.zeros((tail_rows(rows), LANES), jnp.bfloat16)


def far(owners, firsts, main, crossing):
    rows = crossing[0].shape[0]
    block = rows // 2
    half_blocks = 2 * owners
    pair = jax.ShapeDtypeStruct((rows + tail_rows(rows), LANES), jnp.bfloat16)
    return pl.pallas_call(
        functools.partial(far_kernel, owners),
        out_shape=[pair] * owners,
        in_specs=[VMEM] * (owners + 2),
        out_specs=[VMEM] * owners,
        scratch_shapes=[
            pltpu.VMEM(((half_blocks + 2) * block, LANES), jnp.bfloat16),
            pltpu.VMEM((owners, rows, LANES), jnp.bfloat16),
            pltpu.VMEM((block, firsts.shape[1] - block), jnp.bfloat16),
        ],
        compiler_params=params(),
        cost_estimate=cost(1 << 20, 1 << 16),
        name="far",
    )(firsts, main, *crossing)


def adjoints_kernel(owners, key, value, cot, *refs):
    early, late = refs[:owners], refs[owners : 2 * owners]
    query_adj, key_adj, value_adj = refs[2 * owners :]
    rows = key.shape[0]
    q, upper = whereabouts(owners)
    for k in range(owners):
        lanes = pl.ds(pl.multiple_of((q ^ k) * LANES, LANES), LANES)
        first, second = early[k][...], late[k][:rows, :]
        mixed = jnp.where(upper == 1, second, first)
        back = jnp.where(upper == 1, first, second)
        query_adj[:, lanes] = f32_product(cot[:, lanes], mixed).astype(jnp.bfloat16)
        key_adj[:, lanes] = f32_product(back, value[:, lanes]).astype(jnp.bfloat16)
        value_adj[:, lanes] = f32_product(back, key[:, lanes]).astype(jnp.bfloat16)


def adjoints(owners, key, value, cot, early, late):
    rows, channels = key.shape
    width = channels // owners
    if width == LANES:
        return pl.pallas_call(
            functools.partial(adjoints_kernel, owners),
            out_shape=[jax.ShapeDtypeStruct((rows, channels), jnp.bfloat16)] * 3,
            in_specs=[VMEM] * (3 + 2 * owners),
            out_specs=[VMEM] * 3,
            compiler_params=params(),
            name="adjoints",
        )(key, value, cot, *early, *late)
    q, upper = whereabouts(owners)
    both = jnp.zeros((2, rows, channels), jnp.bfloat16)
    for k in range(owners):
        pair = jnp.stack([early[k][:, :width], late[k][:rows, :width]])
        both = lax.dynamic_update_slice_in_dim(both, pair, (q ^ k) * width, 2)
    mixed = jnp.where(upper == 1, both[1], both[0])
    back = jnp.where(upper == 1, both[0], both[1])
    return tuple(
        f32_product(left, right).astype(jnp.bfloat16)
        for left, right in ((cot, mixed), (back, value), (back, key))
    )


def on_device(size, ch_size, query, key, value, filters, cot):
    rows, channels = query.shape
    groups, seq = filters.shape
    owners = size // 2
    q, upper = whereabouts(owners)
    group = lax.axis_index("ch") * channels // GW
    sharing = GW // channels

    def swap(array, axis, count, bits):
        return lax.ppermute(array, axis, [(i, i ^ bits) for i in range(count)])

    def exchange(parts):
        return [parts[0]] + [swap(parts[k], "ctx", size, k) for k in range(1, owners)]

    pairs, own = split_streams(owners, key, value, query, cot)
    halves = exchange(pairs)
    crossing = [own] + [lax.dynamic_index_in_dim(pair, upper, 0, keepdims=False) for pair in halves[1:]]
    crossing = [swap(stream, "ctx", size, owners) for stream in crossing]
    taps = lax.dynamic_index_in_dim(filters, group, 0, keepdims=False)
    firsts = table_rows(taps, rows // 2)
    scale = 1.0 / math.sqrt(seq * GW)
    early, main, near_lags = near(owners, scale, firsts, halves)
    begun = crossing[: owners // 2]
    begun, early = lax.optimization_barrier((begun, list(early)))
    crossing[: owners // 2] = begun
    early = exchange(early)

    def over_group(lags):
        bits = 1
        while bits < sharing:
            lags = lags + swap(lags, "ch", ch_size, bits)
            bits *= 2
        return lags

    near_lags = over_group(near_lags.reshape(owners, rows))
    come = lax.ppermute(near_lags, "ctx", [(i + owners, i) for i in range(owners)])
    near_lags = jnp.where(upper == 1, 0.0, near_lags + come)
    lags = over_group(far_lags(owners, scale, halves, crossing).reshape(owners, rows)) + near_lags
    parts = far(owners, firsts, main, crossing)
    parts, early[1] = lax.optimization_barrier((list(parts), early[1]))
    filled = [parts[0]]
    for k in range(1, owners):
        tail = to_tail(lax.dynamic_index_in_dim(lags, q ^ k, 0, keepdims=False), rows)
        filled.append(lax.dynamic_update_slice(parts[k], tail, (rows, 0)))
    parts = exchange(filled)
    outs = adjoints(owners, key, value, cot, early, parts)
    mine = lax.dynamic_index_in_dim(lags, q, 0, keepdims=False)
    mine = mine + sum(from_tail(part, rows) for part in parts[1:])
    here = jnp.arange(groups, dtype=jnp.int32)[:, None] == group
    bits = sharing
    spread = jnp.where(here, mine[None, :], 0.0)
    while bits < ch_size:
        spread = spread + swap(spread, "ch", ch_size, bits)
        bits *= 2
    return (*outs, spread)


def solution(mesh):
    return jax.shard_map(
        functools.partial(on_device, mesh.shape["ctx"], mesh.shape["ch"]),
        mesh=mesh,
        in_specs=(P("ctx", "ch"), P("ctx", "ch"), P("ctx", "ch"), P(), P("ctx", "ch")),
        out_specs=(P("ctx", "ch"), P("ctx", "ch"), P("ctx", "ch"), P(None, "ctx")),
        check_vma=False,
    )
```

```python
import functools
import math

import jax
import jax.numpy as jnp
from jax import lax
from jax.experimental import pallas as pl
from jax.experimental.pallas import tpu as pltpu
from jax.sharding import PartitionSpec as P

GW = 1024
LANES = 128
VMEM_LIMIT = 13 * 1024 * 1024
WHOLE_VMEM = 60 * 1024 * 1024
VMEM = pl.BlockSpec(memory_space=pltpu.VMEM)
ANY = pl.BlockSpec(memory_space=pl.ANY)


def params(limit=VMEM_LIMIT):
    return pltpu.CompilerParams(vmem_limit_bytes=limit)


def whereabouts(owners):
    me = lax.axis_index("ctx")
    return me % owners, me // owners


def f32_product(left, right):
    return left.astype(jnp.float32) * right.astype(jnp.float32)


def cost(flops, moved):
    return pl.CostEstimate(flops=2 * flops, bytes_accessed=moved, transcendentals=0)


def split_kernel(owners, *refs):
    streams, outs, held, sems = refs[:4], refs[4 : 5 + owners], refs[-2], refs[-1]
    q, upper = whereabouts(owners)
    rows = streams[0].shape[0]
    pieces = held.shape[1]
    span = rows // pieces
    copies = []
    for p in range(pieces):
        for i in range(4):
            copy = pltpu.make_async_copy(
                streams[i].at[pl.ds(p * span, span), :], held.at[i, p], sems.at[i, p]
            )
            copy.start()
            copies.append(copy)
    for p in range(pieces):
        for copy in copies[4 * p : 4 * p + 4]:
            copy.wait()
        here = slice(p * span, (p + 1) * span)
        for k in range(owners):
            lanes = pl.ds(pl.multiple_of((q ^ k) * LANES, LANES), LANES)
            key, value, query, cot = (held[i, p, :, lanes] for i in range(4))
            product = f32_product(key, value).astype(jnp.bfloat16)
            gated = f32_product(cot, query).astype(jnp.bfloat16)
            outs[k][0, here, :] = product
            outs[k][1, here, :] = gated
            if k == 0:
                outs[owners][here, :] = jnp.where(upper == 1, gated, product)


def split_streams(owners, key, value, query, cot):
    rows, channels = key.shape
    width = channels // owners
    if width == LANES:
        pair = jax.ShapeDtypeStruct((2, rows, LANES), jnp.bfloat16)
        single = jax.ShapeDtypeStruct((rows, LANES), jnp.bfloat16)
        outs = pl.pallas_call(
            functools.partial(split_kernel, owners),
            out_shape=[pair] * owners + [single],
            in_specs=[ANY] * 4,
            out_specs=[VMEM] * (owners + 1),
            scratch_shapes=[
                pltpu.VMEM((4, 4, rows // 4, channels), jnp.bfloat16),
                pltpu.SemaphoreType.DMA((4, 4)),
            ],
            compiler_params=params(WHOLE_VMEM),
            name="split_streams",
        )(key, value, query, cot)
        return outs[:owners], outs[owners]
    q, upper = whereabouts(owners)
    product = f32_product(key, value).astype(jnp.bfloat16)
    gated = f32_product(cot, query).astype(jnp.bfloat16)
    both = jnp.stack([product, gated]).reshape(2, rows, owners, width)
    both = jnp.pad(both, ((0, 0), (0, 0), (0, 0), (0, LANES - width)))
    pairs = [lax.dynamic_index_in_dim(both, q ^ k, 2, keepdims=False) for k in range(owners)]
    return pairs, jnp.where(upper == 1, pairs[0][1], pairs[0][0])


def fill_table(row, out):
    block, seq = out.shape
    width = row.shape[1]
    sub = lax.broadcasted_iota(jnp.int32, (8, width), 0)
    eight = jnp.broadcast_to(row, (8, width))
    for bit in (1, 2, 4):
        eight = jnp.where((sub & bit) != 0, pltpu.roll(eight, bit, 1), eight)
    for start in range(0, block, 16):
        low = pltpu.roll(eight, start, 1) if start else eight
        high = pltpu.roll(eight, start + 8, 1)
        both = jnp.concatenate([low[:, :seq], high[:, :seq]], axis=0)
        out[start : start + 16, :] = both.astype(jnp.bfloat16)


def table_rows(taps, block):
    zeros = jnp.zeros((block,), jnp.float32)
    taps = taps.astype(jnp.float32)
    down = jnp.concatenate([taps[::-1], zeros])
    down = jnp.concatenate([down[block - 1 :], down[: block - 1]])
    return jnp.stack([down, jnp.concatenate([taps, zeros])])


def tail_rows(rows):
    return -(-2 * rows // (16 * LANES)) * 16


def to_tail(lags, rows):
    high = lax.reduce_precision(lags, 8, 7)
    low = (lags - high).astype(jnp.bfloat16)
    high = high.astype(jnp.bfloat16)
    flat = jnp.concatenate([high.reshape(-1, LANES), low.reshape(-1, LANES)])
    return jnp.pad(flat, ((0, tail_rows(rows) - flat.shape[0]), (0, 0)))


def from_tail(part, rows):
    count = rows // LANES
    pairs = part[rows : rows + 2 * count].astype(jnp.float32)
    return (pairs[:count] + pairs[count:]).reshape(rows)


def fold_diagonals(sums, out):
    blocks, block = sums.shape[0], sums.shape[1]
    steps = block // LANES

    def diagonal(lag):
        total = None
        for a in range(steps):
            b = lag + a
            if b // steps < blocks:
                rows = slice(a * LANES, (a + 1) * LANES)
                cols = slice((b % steps) * LANES, (b % steps + 1) * LANES)
                tile = sums[b // steps, rows, cols]
                total = tile if total is None else total + tile
        return jnp.zeros((LANES, LANES), jnp.float32) if total is None else total

    row = lax.broadcasted_iota(jnp.int32, (LANES, LANES), 0)
    col = lax.broadcasted_iota(jnp.int32, (LANES, LANES), 1)
    sub = lax.broadcasted_iota(jnp.int32, (8, LANES), 0)
    current = diagonal(0)
    for lag in range(out.shape[0]):
        after = diagonal(lag + 1)
        mixed = jnp.where(col >= row, current, after)
        eight = mixed[:8]
        for m in range(1, LANES // 8):
            eight = eight + pltpu.roll(mixed[8 * m : 8 * m + 8], LANES - 8 * m, 1)
        for bit in (1, 2, 4):
            eight = jnp.where((sub & bit) != 0, pltpu.roll(eight, LANES - bit, 1), eight)
        out[lag : lag + 1, :] = jnp.sum(eight, axis=0, keepdims=True)
        current = after


def cross_rows(left, right):
    return lax.dot_general(
        left, right, (((1,), (1,)), ((), ())), preferred_element_type=jnp.float32
    )


def far_lags_kernel(owners, scale, *refs):
    halves, crossing = refs[:owners], refs[owners : 2 * owners]
    out, lane_blocks, sums = refs[2 * owners :]
    q, upper = whereabouts(owners)
    block = halves[0].shape[1] // 2
    half_blocks = 2 * owners
    for k in range(owners):
        for part in range(2):
            rows = slice(part * block, (part + 1) * block)
            lanes = pl.ds(pl.multiple_of((2 * (q ^ k) + part) * LANES, LANES), LANES)
            lane_blocks[upper, :, lanes] = halves[k][upper, rows, :]
            lane_blocks[1 - upper, :, lanes] = crossing[k][rows, :]
    sums[half_blocks * upper] = jnp.zeros((block, block), jnp.float32)
    for i in range(half_blocks):
        count = (half_blocks - i) * LANES
        left = pl.ds(pl.multiple_of((1 - upper) * i * LANES, LANES), count)
        right = pl.ds(pl.multiple_of(upper * i * LANES, LANES), count)
        lag = jnp.where(upper == 1, i, half_blocks - i)
        sums[lag] = cross_rows(lane_blocks[0, :, left], lane_blocks[1, :, right])
    fold_diagonals(sums, out)
    out[...] *= scale


def far_lags(owners, scale, halves, crossing):
    block = halves[0].shape[1] // 2
    half_blocks = 2 * owners
    return pl.pallas_call(
        functools.partial(far_lags_kernel, owners, scale),
        out_shape=jax.ShapeDtypeStruct((half_blocks * block // LANES, LANES), jnp.float32),
        in_specs=[VMEM] * (2 * owners),
        out_specs=VMEM,
        scratch_shapes=[
            pltpu.VMEM((2, block, half_blocks * LANES), jnp.bfloat16),
            pltpu.VMEM((half_blocks + 1, block, block), jnp.float32),
        ],
        compiler_params=params(),
        cost_estimate=cost(half_blocks * half_blocks * block * block * LANES // 2, 2 << 20),
        name="far_lags",
    )(*halves, *crossing)


def near_kernel(owners, scale, firsts, *refs):
    halves = refs[:owners]
    early = refs[owners : 2 * owners]
    main, near_lags, results, streams, lane_blocks, sums, tables = refs[2 * owners :]
    for which in range(2):
        fill_table(firsts[which : which + 1, :], tables.at[which])
    q, upper = whereabouts(owners)
    rows = halves[0].shape[1]
    block = rows // 2
    half_blocks = 2 * owners
    zeros = jnp.zeros((2, block, LANES), jnp.bfloat16)
    streams[:, :block] = zeros
    streams[:, (half_blocks + 1) * block :] = zeros
    for k in range(owners):
        start = pl.multiple_of(block + (q ^ k) * rows, block)
        streams[:, pl.ds(start, rows), :] = halves[k][...]
        for part in range(2):
            lanes = pl.ds(pl.multiple_of((2 * (q ^ k) + part) * LANES, LANES), LANES)
            lane_blocks[:, :, lanes] = halves[k][:, part * block : (part + 1) * block, :]
    for which in range(2):
        for i in range(owners):
            depth = (2 * i + 2) * block
            if which == 0:
                window = tables[0, :, tables.shape[2] - depth :]
                first, to = 0, i
            else:
                window = tables[1, :, :depth]
                first, to = (half_blocks - 1 - 2 * i) * block, owners - 1 - i
            pair = jnp.concatenate(
                [
                    streams[which, first : first + depth, :],
                    streams[which, first + block : first + block + depth, :],
                ],
                axis=1,
            )
            got = jnp.dot(window, pair, preferred_element_type=jnp.float32)
            results[which, to, :block, :] = got[:, :LANES]
            results[which, to, block:, :] = got[:, LANES:]
    for k in range(owners):
        early[k][...] = results[upper, q ^ k].astype(jnp.bfloat16)
    main[...] = results[1 - upper]
    for lag in range(half_blocks):
        count = (half_blocks - lag) * LANES
        sums[lag] = cross_rows(
            lane_blocks[0, :, :count], lane_blocks[1, :, lag * LANES : lag * LANES + count]
        )
    fold_diagonals(sums, near_lags)
    near_lags[...] *= scale


def near(owners, scale, firsts, halves):
    rows = halves[0].shape[1]
    block = rows // 2
    half_blocks = 2 * owners
    single = jax.ShapeDtypeStruct((rows, LANES), jnp.bfloat16)
    outs = pl.pallas_call(
        functools.partial(near_kernel, owners, scale),
        out_shape=[single] * owners
        + [
            jax.ShapeDtypeStruct((owners, rows, LANES), jnp.float32),
            jax.ShapeDtypeStruct((half_blocks * block // LANES, LANES), jnp.float32),
        ],
        in_specs=[VMEM] * (owners + 1),
        out_specs=[VMEM] * (owners + 2),
        scratch_shapes=[
            pltpu.VMEM((2, owners, rows, LANES), jnp.float32),
            pltpu.VMEM((2, (half_blocks + 2) * block, LANES), jnp.bfloat16),
            pltpu.VMEM((2, block, half_blocks * LANES), jnp.bfloat16),
            pltpu.VMEM((half_blocks, block, block), jnp.float32),
            pltpu.VMEM((2, block, firsts.shape[1] - block), jnp.bfloat16),
        ],
        compiler_params=params(),
        cost_estimate=cost(3 * half_blocks * half_blocks * block * block * LANES, 8 << 20),
        name="near",
    )(firsts, *halves)
    return outs[:owners], outs[owners], outs[owners + 1]


def far_kernel(owners, firsts, main, *refs):
    crossing, outs = refs[:owners], refs[owners : 2 * owners]
    stream, results, table = refs[2 * owners :]
    q, upper = whereabouts(owners)
    rows = crossing[0].shape[0]
    block = rows // 2
    half_blocks = 2 * owners
    zeros = jnp.zeros((block, LANES), jnp.bfloat16)
    stream[:block] = zeros
    stream[(half_blocks + 1) * block :] = zeros
    for k in range(owners):
        start = pl.multiple_of(block + (q ^ k) * rows, block)
        stream[pl.ds(start, rows), :] = crossing[k][...]
    fill_table(firsts[pl.ds(1 - upper, 1), :], table)
    depth = (half_blocks + 1) * block
    pair = jnp.concatenate([stream[:depth, :], stream[block : block + depth, :]], axis=1)
    for group in range(0, owners, 4):
        several = range(group, min(group + 4, owners))
        windows = []
        for i in several:
            start = jnp.where(upper == 1, half_blocks - 2 - 2 * i, 1 + 2 * i) * block
            windows.append(table[:, pl.ds(pl.multiple_of(start, block), depth)])
        all_got = jnp.dot(
            jnp.concatenate(windows, axis=0), pair, preferred_element_type=jnp.float32
        )
        for n, i in enumerate(several):
            got = all_got[n * block : (n + 1) * block, :]
            to = jnp.where(upper == 1, i, owners - 1 - i)
            low = main[to, :block, :] + got[:, :LANES]
            high = main[to, block:, :] + got[:, LANES:]
            results[to, :block, :] = low.astype(jnp.bfloat16)
            results[to, block:, :] = high.astype(jnp.bfloat16)
    for k in range(owners):
        outs[k][:rows, :] = results[q ^ k]
        outs[k][rows:, :] = jnp.zeros((tail_rows(rows), LANES), jnp.bfloat16)


def far(owners, firsts, main, crossing):
    rows = crossing[0].shape[0]
    block = rows // 2
    half_blocks = 2 * owners
    pair = jax.ShapeDtypeStruct((rows + tail_rows(rows), LANES), jnp.bfloat16)
    return pl.pallas_call(
        functools.partial(far_kernel, owners),
        out_shape=[pair] * owners,
        in_specs=[VMEM] * (owners + 2),
        out_specs=[VMEM] * owners,
        scratch_shapes=[
            pltpu.VMEM(((half_blocks + 2) * block, LANES), jnp.bfloat16),
            pltpu.VMEM((owners, rows, LANES), jnp.bfloat16),
            pltpu.VMEM((block, firsts.shape[1] - block), jnp.bfloat16),
        ],
        compiler_params=params(VMEM_LIMIT * max(1, owners // 4)),
        name="far",
    )(firsts, main, *crossing)


def adjoints_kernel(owners, key, value, cot, *refs):
    early, late = refs[:owners], refs[owners : 2 * owners]
    query_adj, key_adj, value_adj = refs[2 * owners :]
    rows = key.shape[0]
    q, upper = whereabouts(owners)
    for k in range(owners):
        lanes = pl.ds(pl.multiple_of((q ^ k) * LANES, LANES), LANES)
        first, second = early[k][...], late[k][:rows, :]
        mixed = jnp.where(upper == 1, second, first)
        back = jnp.where(upper == 1, first, second)
        query_adj[:, lanes] = f32_product(cot[:, lanes], mixed).astype(jnp.bfloat16)
        key_adj[:, lanes] = f32_product(back, value[:, lanes]).astype(jnp.bfloat16)
        value_adj[:, lanes] = f32_product(back, key[:, lanes]).astype(jnp.bfloat16)


def adjoints(owners, key, value, cot, early, late):
    rows, channels = key.shape
    width = channels // owners
    if width == LANES:
        return pl.pallas_call(
            functools.partial(adjoints_kernel, owners),
            out_shape=[jax.ShapeDtypeStruct((rows, channels), jnp.bfloat16)] * 3,
            in_specs=[VMEM] * (3 + 2 * owners),
            out_specs=[VMEM] * 3,
            compiler_params=params(),
            name="adjoints",
        )(key, value, cot, *early, *late)
    q, upper = whereabouts(owners)
    both = jnp.zeros((2, rows, channels), jnp.bfloat16)
    for k in range(owners):
        pair = jnp.stack([early[k][:, :width], late[k][:rows, :width]])
        both = lax.dynamic_update_slice_in_dim(both, pair, (q ^ k) * width, 2)
    mixed = jnp.where(upper == 1, both[1], both[0])
    back = jnp.where(upper == 1, both[0], both[1])
    return tuple(
        f32_product(left, right).astype(jnp.bfloat16)
        for left, right in ((cot, mixed), (back, value), (back, key))
    )


def on_device(size, ch_size, query, key, value, filters, cot):
    rows, channels = query.shape
    groups, seq = filters.shape
    owners = size // 2
    q, upper = whereabouts(owners)
    group = lax.axis_index("ch") * channels // GW
    sharing = GW // channels

    def swap(array, axis, count, bits):
        return lax.ppermute(array, axis, [(i, i ^ bits) for i in range(count)])

    def exchange(parts, order):
        come = {k: swap(parts[k], "ctx", size, k) for k in order}
        return [parts[0]] + [come[k] for k in range(1, owners)]

    close, distant = range(1, owners // 2), range(owners // 2, owners)

    pairs, own = split_streams(owners, key, value, query, cot)
    halves = exchange(pairs, [*distant, *close])
    crossing = [own] + [lax.dynamic_index_in_dim(pair, upper, 0, keepdims=False) for pair in halves[1:]]
    crossing = [swap(stream, "ctx", size, owners) for stream in crossing]
    taps = lax.dynamic_index_in_dim(filters, group, 0, keepdims=False)
    firsts = table_rows(taps, rows // 2)
    scale = 1.0 / math.sqrt(seq * GW)
    early, main, near_lags = near(owners, scale, firsts, halves)
    early = exchange(early, [*close, *distant])

    def over_group(lags):
        bits = 1
        while bits < sharing:
            lags = lags + swap(lags, "ch", ch_size, bits)
            bits *= 2
        return lags

    near_lags = over_group(near_lags.reshape(owners, rows))
    come = lax.ppermute(near_lags, "ctx", [(i + owners, i) for i in range(owners)])
    near_lags = jnp.where(upper == 1, 0.0, near_lags + come)
    lags = over_group(far_lags(owners, scale, halves, crossing).reshape(owners, rows)) + near_lags
    parts = far(owners, firsts, main, crossing)
    for k in distant:
        parts, early[k] = lax.optimization_barrier((list(parts), early[k]))
    filled = [parts[0]]
    for k in range(1, owners):
        tail = to_tail(lax.dynamic_index_in_dim(lags, q ^ k, 0, keepdims=False), rows)
        filled.append(lax.dynamic_update_slice(parts[k], tail, (rows, 0)))
    parts = exchange(filled, [*close, *distant])
    mine = lax.dynamic_index_in_dim(lags, q, 0, keepdims=False)
    mine = mine + sum(from_tail(part, rows) for part in parts[1:])
    here = jnp.arange(groups, dtype=jnp.int32)[:, None] == group
    bits = sharing
    spread = jnp.where(here, mine[None, :], 0.0)
    while bits < ch_size:
        spread = spread + swap(spread, "ch", ch_size, bits)
        bits *= 2
    outs = adjoints(owners, key, value, cot, early, parts)
    return (*outs, spread)


def solution(mesh):
    return jax.shard_map(
        functools.partial(on_device, mesh.shape["ctx"], mesh.shape["ch"]),
        mesh=mesh,
        in_specs=(P("ctx", "ch"), P("ctx", "ch"), P("ctx", "ch"), P(), P("ctx", "ch")),
        out_specs=(P("ctx", "ch"), P("ctx", "ch"), P("ctx", "ch"), P(None, "ctx")),
        check_vma=False,
    )
```

```python
import functools
import math

import jax
import jax.numpy as jnp
from jax import lax
from jax.experimental import pallas as pl
from jax.experimental.pallas import tpu as pltpu
from jax.sharding import PartitionSpec as P

GW = 1024
LANES = 128
VMEM_LIMIT = 13 * 1024 * 1024
WHOLE_VMEM = 60 * 1024 * 1024
VMEM = pl.BlockSpec(memory_space=pltpu.VMEM)
ANY = pl.BlockSpec(memory_space=pl.ANY)


def params(limit=VMEM_LIMIT):
    return pltpu.CompilerParams(vmem_limit_bytes=limit)


def whereabouts(owners):
    me = lax.axis_index("ctx")
    return me % owners, me // owners


def f32_product(left, right):
    return left.astype(jnp.float32) * right.astype(jnp.float32)


def cost(flops, moved):
    return pl.CostEstimate(flops=2 * flops, bytes_accessed=moved, transcendentals=0)


def split_kernel(owners, *refs):
    streams, outs, held, sems = refs[:4], refs[4 : 5 + owners], refs[-2], refs[-1]
    q, upper = whereabouts(owners)
    rows = streams[0].shape[0]
    pieces = held.shape[1]
    span = rows // pieces
    copies = []
    for p in range(pieces):
        for i in range(4):
            copy = pltpu.make_async_copy(
                streams[i].at[pl.ds(p * span, span), :], held.at[i, p], sems.at[i, p]
            )
            copy.start()
            copies.append(copy)
    for p in range(pieces):
        for copy in copies[4 * p : 4 * p + 4]:
            copy.wait()
        here = slice(p * span, (p + 1) * span)
        for k in range(owners):
            lanes = pl.ds(pl.multiple_of((q ^ k) * LANES, LANES), LANES)
            key, value, query, cot = (held[i, p, :, lanes] for i in range(4))
            product = f32_product(key, value).astype(jnp.bfloat16)
            gated = f32_product(cot, query).astype(jnp.bfloat16)
            outs[k][0, here, :] = product
            outs[k][1, here, :] = gated
            if k == 0:
                outs[owners][here, :] = jnp.where(upper == 1, gated, product)


def split_streams(owners, key, value, query, cot):
    rows, channels = key.shape
    width = channels // owners
    if width == LANES:
        pair = jax.ShapeDtypeStruct((2, rows, LANES), jnp.bfloat16)
        single = jax.ShapeDtypeStruct((rows, LANES), jnp.bfloat16)
        outs = pl.pallas_call(
            functools.partial(split_kernel, owners),
            out_shape=[pair] * owners + [single],
            in_specs=[ANY] * 4,
            out_specs=[VMEM] * (owners + 1),
            scratch_shapes=[
                pltpu.VMEM((4, 4, rows // 4, channels), jnp.bfloat16),
                pltpu.SemaphoreType.DMA((4, 4)),
            ],
            compiler_params=params(WHOLE_VMEM),
            name="split_streams",
        )(key, value, query, cot)
        return outs[:owners], outs[owners]
    q, upper = whereabouts(owners)
    product = f32_product(key, value).astype(jnp.bfloat16)
    gated = f32_product(cot, query).astype(jnp.bfloat16)
    both = jnp.stack([product, gated]).reshape(2, rows, owners, width)
    both = jnp.pad(both, ((0, 0), (0, 0), (0, 0), (0, LANES - width)))
    pairs = [lax.dynamic_index_in_dim(both, q ^ k, 2, keepdims=False) for k in range(owners)]
    return pairs, jnp.where(upper == 1, pairs[0][1], pairs[0][0])


def fill_table(row, out):
    block, seq = out.shape
    width = row.shape[1]
    sub = lax.broadcasted_iota(jnp.int32, (8, width), 0)
    eight = jnp.broadcast_to(row, (8, width))
    for bit in (1, 2, 4):
        eight = jnp.where((sub & bit) != 0, pltpu.roll(eight, bit, 1), eight)
    for start in range(0, block, 16):
        low = pltpu.roll(eight, start, 1) if start else eight
        high = pltpu.roll(eight, start + 8, 1)
        both = jnp.concatenate([low[:, :seq], high[:, :seq]], axis=0)
        out[start : start + 16, :] = both.astype(jnp.bfloat16)


def table_rows(taps, block):
    zeros = jnp.zeros((block,), jnp.float32)
    taps = taps.astype(jnp.float32)
    down = jnp.concatenate([taps[::-1], zeros])
    down = jnp.concatenate([down[block - 1 :], down[: block - 1]])
    return jnp.stack([down, jnp.concatenate([taps, zeros])])


def tail_rows(rows):
    return -(-2 * rows // (16 * LANES)) * 16


def to_tail(lags, rows):
    high = lax.reduce_precision(lags, 8, 7)
    low = (lags - high).astype(jnp.bfloat16)
    high = high.astype(jnp.bfloat16)
    flat = jnp.concatenate([high.reshape(-1, LANES), low.reshape(-1, LANES)])
    return jnp.pad(flat, ((0, tail_rows(rows) - flat.shape[0]), (0, 0)))


def from_tail(part, rows):
    count = rows // LANES
    pairs = part[rows : rows + 2 * count].astype(jnp.float32)
    return (pairs[:count] + pairs[count:]).reshape(rows)


def fold_diagonals(sums, out):
    blocks, block = sums.shape[0], sums.shape[1]
    steps = block // LANES

    def diagonal(lag):
        total = None
        for a in range(steps):
            b = lag + a
            if b // steps < blocks:
                rows = slice(a * LANES, (a + 1) * LANES)
                cols = slice((b % steps) * LANES, (b % steps + 1) * LANES)
                tile = sums[b // steps, rows, cols]
                total = tile if total is None else total + tile
        return jnp.zeros((LANES, LANES), jnp.float32) if total is None else total

    row = lax.broadcasted_iota(jnp.int32, (LANES, LANES), 0)
    col = lax.broadcasted_iota(jnp.int32, (LANES, LANES), 1)
    sub = lax.broadcasted_iota(jnp.int32, (8, LANES), 0)
    current = diagonal(0)
    for lag in range(out.shape[0]):
        after = diagonal(lag + 1)
        mixed = jnp.where(col >= row, current, after)
        eight = mixed[:8]
        for m in range(1, LANES // 8):
            eight = eight + pltpu.roll(mixed[8 * m : 8 * m + 8], LANES - 8 * m, 1)
        for bit in (1, 2, 4):
            eight = jnp.where((sub & bit) != 0, pltpu.roll(eight, LANES - bit, 1), eight)
        out[lag : lag + 1, :] = jnp.sum(eight, axis=0, keepdims=True)
        current = after


def cross_rows(left, right):
    return lax.dot_general(
        left, right, (((1,), (1,)), ((), ())), preferred_element_type=jnp.float32
    )


def far_lags_kernel(owners, scale, *refs):
    halves, crossing = refs[:owners], refs[owners : 2 * owners]
    out, lane_blocks, sums = refs[2 * owners :]
    q, upper = whereabouts(owners)
    block = halves[0].shape[1] // 2
    half_blocks = 2 * owners
    for k in range(owners):
        for part in range(2):
            rows = slice(part * block, (part + 1) * block)
            lanes = pl.ds(pl.multiple_of((2 * (q ^ k) + part) * LANES, LANES), LANES)
            lane_blocks[upper, :, lanes] = halves[k][upper, rows, :]
            lane_blocks[1 - upper, :, lanes] = crossing[k][rows, :]
    sums[half_blocks * upper] = jnp.zeros((block, block), jnp.float32)
    for i in range(half_blocks):
        count = (half_blocks - i) * LANES
        left = pl.ds(pl.multiple_of((1 - upper) * i * LANES, LANES), count)
        right = pl.ds(pl.multiple_of(upper * i * LANES, LANES), count)
        lag = jnp.where(upper == 1, i, half_blocks - i)
        sums[lag] = cross_rows(lane_blocks[0, :, left], lane_blocks[1, :, right])
    fold_diagonals(sums, out)
    out[...] *= scale


def far_lags(owners, scale, halves, crossing):
    block = halves[0].shape[1] // 2
    half_blocks = 2 * owners
    return pl.pallas_call(
        functools.partial(far_lags_kernel, owners, scale),
        out_shape=jax.ShapeDtypeStruct((half_blocks * block // LANES, LANES), jnp.float32),
        in_specs=[VMEM] * (2 * owners),
        out_specs=VMEM,
        scratch_shapes=[
            pltpu.VMEM((2, block, half_blocks * LANES), jnp.bfloat16),
            pltpu.VMEM((half_blocks + 1, block, block), jnp.float32),
        ],
        compiler_params=params(),
        cost_estimate=cost(half_blocks * half_blocks * block * block * LANES // 2, 2 << 20),
        name="far_lags",
    )(*halves, *crossing)


def near_kernel(owners, scale, firsts, *refs):
    halves = refs[:owners]
    early = refs[owners : 2 * owners]
    main, near_lags, results, streams, lane_blocks, sums, tables = refs[2 * owners :]
    for which in range(2):
        fill_table(firsts[which : which + 1, :], tables.at[which])
    q, upper = whereabouts(owners)
    rows = halves[0].shape[1]
    block = rows // 2
    half_blocks = 2 * owners
    zeros = jnp.zeros((2, block, LANES), jnp.bfloat16)
    streams[:, :block] = zeros
    streams[:, (half_blocks + 1) * block :] = zeros
    for k in range(owners):
        start = pl.multiple_of(block + (q ^ k) * rows, block)
        streams[:, pl.ds(start, rows), :] = halves[k][...]
        for part in range(2):
            lanes = pl.ds(pl.multiple_of((2 * (q ^ k) + part) * LANES, LANES), LANES)
            lane_blocks[:, :, lanes] = halves[k][:, part * block : (part + 1) * block, :]
    for which in range(2):
        for i in range(owners):
            depth = (2 * i + 2) * block
            if which == 0:
                window = tables[0, :, tables.shape[2] - depth :]
                first, to = 0, i
            else:
                window = tables[1, :, :depth]
                first, to = (half_blocks - 1 - 2 * i) * block, owners - 1 - i
            pair = jnp.concatenate(
                [
                    streams[which, first : first + depth, :],
                    streams[which, first + block : first + block + depth, :],
                ],
                axis=1,
            )
            got = jnp.dot(window, pair, preferred_element_type=jnp.float32)
            results[which, to, :block, :] = got[:, :LANES]
            results[which, to, block:, :] = got[:, LANES:]
    for k in range(owners):
        early[k][...] = results[upper, q ^ k].astype(jnp.bfloat16)
    main[...] = results[1 - upper]
    for lag in range(half_blocks):
        count = (half_blocks - lag) * LANES
        sums[lag] = cross_rows(
            lane_blocks[0, :, :count], lane_blocks[1, :, lag * LANES : lag * LANES + count]
        )
    fold_diagonals(sums, near_lags)
    near_lags[...] *= scale


def near(owners, scale, firsts, halves):
    rows = halves[0].shape[1]
    block = rows // 2
    half_blocks = 2 * owners
    single = jax.ShapeDtypeStruct((rows, LANES), jnp.bfloat16)
    outs = pl.pallas_call(
        functools.partial(near_kernel, owners, scale),
        out_shape=[single] * owners
        + [
            jax.ShapeDtypeStruct((owners, rows, LANES), jnp.float32),
            jax.ShapeDtypeStruct((half_blocks * block // LANES, LANES), jnp.float32),
        ],
        in_specs=[VMEM] * (owners + 1),
        out_specs=[VMEM] * (owners + 2),
        scratch_shapes=[
            pltpu.VMEM((2, owners, rows, LANES), jnp.float32),
            pltpu.VMEM((2, (half_blocks + 2) * block, LANES), jnp.bfloat16),
            pltpu.VMEM((2, block, half_blocks * LANES), jnp.bfloat16),
            pltpu.VMEM((half_blocks, block, block), jnp.float32),
            pltpu.VMEM((2, block, firsts.shape[1] - block), jnp.bfloat16),
        ],
        compiler_params=params(),
        cost_estimate=cost(3 * half_blocks * half_blocks * block * block * LANES, 8 << 20),
        name="near",
    )(firsts, *halves)
    return outs[:owners], outs[owners], outs[owners + 1]


def far_kernel(owners, firsts, main, *refs):
    crossing, outs = refs[:owners], refs[owners : 2 * owners]
    stream, results, table = refs[2 * owners :]
    q, upper = whereabouts(owners)
    rows = crossing[0].shape[0]
    block = rows // 2
    half_blocks = 2 * owners
    zeros = jnp.zeros((block, LANES), jnp.bfloat16)
    stream[:block] = zeros
    stream[(half_blocks + 1) * block :] = zeros
    for k in range(owners):
        start = pl.multiple_of(block + (q ^ k) * rows, block)
        stream[pl.ds(start, rows), :] = crossing[k][...]
    fill_table(firsts[pl.ds(1 - upper, 1), :], table)
    depth = (half_blocks + 1) * block
    pair = jnp.concatenate([stream[:depth, :], stream[block : block + depth, :]], axis=1)
    for group in range(0, owners, 4):
        several = range(group, min(group + 4, owners))
        windows = []
        for i in several:
            start = jnp.where(upper == 1, half_blocks - 2 - 2 * i, 1 + 2 * i) * block
            windows.append(table[:, pl.ds(pl.multiple_of(start, block), depth)])
        all_got = jnp.dot(
            jnp.concatenate(windows, axis=0), pair, preferred_element_type=jnp.float32
        )
        for n, i in enumerate(several):
            got = all_got[n * block : (n + 1) * block, :]
            to = jnp.where(upper == 1, i, owners - 1 - i)
            low = main[to, :block, :] + got[:, :LANES]
            high = main[to, block:, :] + got[:, LANES:]
            results[to, :block, :] = low.astype(jnp.bfloat16)
            results[to, block:, :] = high.astype(jnp.bfloat16)
    for k in range(owners):
        outs[k][:rows, :] = results[q ^ k]
        outs[k][rows:, :] = jnp.zeros((tail_rows(rows), LANES), jnp.bfloat16)


def far(owners, firsts, main, crossing):
    rows = crossing[0].shape[0]
    block = rows // 2
    half_blocks = 2 * owners
    pair = jax.ShapeDtypeStruct((rows + tail_rows(rows), LANES), jnp.bfloat16)
    return pl.pallas_call(
        functools.partial(far_kernel, owners),
        out_shape=[pair] * owners,
        in_specs=[VMEM] * (owners + 2),
        out_specs=[VMEM] * owners,
        scratch_shapes=[
            pltpu.VMEM(((half_blocks + 2) * block, LANES), jnp.bfloat16),
            pltpu.VMEM((owners, rows, LANES), jnp.bfloat16),
            pltpu.VMEM((block, firsts.shape[1] - block), jnp.bfloat16),
        ],
        compiler_params=params(VMEM_LIMIT * max(1, owners // 4)),
        name="far",
    )(firsts, main, *crossing)


def adjoints_kernel(owners, key, value, cot, *refs):
    early, late = refs[:owners], refs[owners : 2 * owners]
    query_adj, key_adj, value_adj = refs[2 * owners :]
    rows = key.shape[0]
    q, upper = whereabouts(owners)
    for k in range(owners):
        lanes = pl.ds(pl.multiple_of((q ^ k) * LANES, LANES), LANES)
        first, second = early[k][...], late[k][:rows, :]
        mixed = jnp.where(upper == 1, second, first)
        back = jnp.where(upper == 1, first, second)
        query_adj[:, lanes] = f32_product(cot[:, lanes], mixed).astype(jnp.bfloat16)
        key_adj[:, lanes] = f32_product(back, value[:, lanes]).astype(jnp.bfloat16)
        value_adj[:, lanes] = f32_product(back, key[:, lanes]).astype(jnp.bfloat16)


def adjoints(owners, key, value, cot, early, late):
    rows, channels = key.shape
    width = channels // owners
    if width == LANES:
        return pl.pallas_call(
            functools.partial(adjoints_kernel, owners),
            out_shape=[jax.ShapeDtypeStruct((rows, channels), jnp.bfloat16)] * 3,
            in_specs=[VMEM] * (3 + 2 * owners),
            out_specs=[VMEM] * 3,
            compiler_params=params(),
            name="adjoints",
        )(key, value, cot, *early, *late)
    q, upper = whereabouts(owners)
    both = jnp.zeros((2, rows, channels), jnp.bfloat16)
    for k in range(owners):
        pair = jnp.stack([early[k][:, :width], late[k][:rows, :width]])
        both = lax.dynamic_update_slice_in_dim(both, pair, (q ^ k) * width, 2)
    mixed = jnp.where(upper == 1, both[1], both[0])
    back = jnp.where(upper == 1, both[0], both[1])
    return tuple(
        f32_product(left, right).astype(jnp.bfloat16)
        for left, right in ((cot, mixed), (back, value), (back, key))
    )


def on_device(size, ch_size, query, key, value, filters, cot):
    rows, channels = query.shape
    groups, seq = filters.shape
    owners = size // 2
    q, upper = whereabouts(owners)
    group = lax.axis_index("ch") * channels // GW
    sharing = GW // channels

    def swap(array, axis, count, bits):
        return lax.ppermute(array, axis, [(i, i ^ bits) for i in range(count)])

    def exchange(parts, order):
        come = {k: swap(parts[k], "ctx", size, k) for k in order}
        return [parts[0]] + [come[k] for k in range(1, owners)]

    close, distant = range(1, owners // 2), range(owners // 2, owners)

    pairs, own = split_streams(owners, key, value, query, cot)
    halves = exchange(pairs, [*distant, *close])
    crossing = [own] + [lax.dynamic_index_in_dim(pair, upper, 0, keepdims=False) for pair in halves[1:]]
    crossing = [swap(stream, "ctx", size, owners) for stream in crossing]
    taps = lax.dynamic_index_in_dim(filters, group, 0, keepdims=False)
    firsts = table_rows(taps, rows // 2)
    scale = 1.0 / math.sqrt(seq * GW)
    early, main, near_lags = near(owners, scale, firsts, halves)
    early = exchange(early, [*close, *distant])

    def over_group(lags):
        bits = 1
        while bits < sharing:
            lags = lags + swap(lags, "ch", ch_size, bits)
            bits *= 2
        return lags

    near_lags = near_lags.reshape(owners, rows)
    come = lax.ppermute(near_lags, "ctx", [(i + owners, i) for i in range(owners)])
    near_lags = jnp.where(upper == 1, 0.0, near_lags + come)
    lags = over_group(far_lags(owners, scale, halves, crossing).reshape(owners, rows) + near_lags)
    parts = far(owners, firsts, main, crossing)
    for k in reversed(distant):
        parts, early[k] = lax.optimization_barrier((list(parts), early[k]))
    filled = [parts[0]]
    for k in range(1, owners):
        tail = to_tail(lax.dynamic_index_in_dim(lags, q ^ k, 0, keepdims=False), rows)
        filled.append(lax.dynamic_update_slice(parts[k], tail, (rows, 0)))
    parts = exchange(filled, [*close, *distant])
    mine = lax.dynamic_index_in_dim(lags, q, 0, keepdims=False)
    mine = mine + sum(from_tail(part, rows) for part in parts[1:])
    here = jnp.arange(groups, dtype=jnp.int32)[:, None] == group
    bits = sharing
    spread = jnp.where(here, mine[None, :], 0.0)
    while bits < ch_size:
        spread = spread + swap(spread, "ch", ch_size, bits)
        bits *= 2
    outs = adjoints(owners, key, value, cot, early, parts)
    return (*outs, spread)


def solution(mesh):
    return jax.shard_map(
        functools.partial(on_device, mesh.shape["ctx"], mesh.shape["ch"]),
        mesh=mesh,
        in_specs=(P("ctx", "ch"), P("ctx", "ch"), P("ctx", "ch"), P(), P("ctx", "ch")),
        out_specs=(P("ctx", "ch"), P("ctx", "ch"), P("ctx", "ch"), P(None, "ctx")),
        check_vma=False,
    )
```
